32 devices in a mesh: group: 2 (over y), along: 8 (over z, x), cross: 2 (over core).
Axes of the slice: x: 2, y: 2, z: 4, core: 2. Of those that a mesh axis runs over, the one named last changes fastest.
Arguments:
- floc_conc: float32 [15, 8, 64, 512], P(None, None, ('group', 'along'), 'cross'), parts along dimension 2, may hold values from 0.05 to 2
- currents: float32 [2, 64, 512], P(None, ('group', 'along'), 'cross'), parts along dimension 1, may hold values from -0.3 to 0.3
- water_depth: float32 [64, 512], P(('group', 'along'), 'cross'), parts along dimension 0, may hold values from 0.5 to 8
- wet_mask: int32 [64, 512], P(('group', 'along'), 'cross'), parts along dimension 0, may hold values 0 or 1
- shear_rate: float32 [8, 64, 512], P(None, ('group', 'along'), 'cross'), parts along dimension 1, may hold values from 0.1 to 1
- aggregation: float32 [15, 15], replicated, may hold values from -1.5 to 1.5
- breakup: float32 [15, 15], replicated, may hold values from -1.5 to 1.5
- settling: float32 [15], replicated, may hold values from 0.05 to 0.4
- erosion: float32 [15], replicated, may hold values from 0.05 to 0.5
- action_density: float32 [36, 16, 32, 256], P(None, None, ('group', 'along', 'cross')), parts along dimension 2, may hold values from 0.1 to 2
- wind_growth: float32 [36, 16], replicated, may hold values from -0.3 to 0.3
Outputs:
- floc_next: float32 [15, 8, 64, 512], P(None, None, ('group', 'along'), 'cross'), parts along dimension 2
- action_next: float32 [36, 16, 32, 256], P(None, None, ('group', 'along', 'cross')), parts along dimension 2
The draws below stay inside these ranges and needn't reach their ends.
There are 2 independent parts, one for each index of `group`. The reference program is written for one: setup_inputs(seed, part) draws one part's arguments, and reference() takes and returns one part's arrays. A program takes and returns all parts, laid end to end along the dimension named above; an argument that names none is the same for every part. Nothing has to cross between parts.
Inputs may be any that keep to these rules, and one draw needn't show every extreme that they name: `wet_mask`: 1 marks a wet ocean cell, 0 a dry one.
All inputs are finite; a program needn't handle non-finite values. No bound on the sum of `wet_mask` on one device may be relied on, other than what follows from the above.
Results may differ from the reference program's by a relative error of at most 0.00017.
Values sent between devices are 32-bit elements; how exact they have to be, the bound alone decides.
A program may use at most 64 MiB of HBM per device.

```python
import math
import jax
import jax.numpy as jnp
from jax import lax

CLASSES = 15
LEVELS = 8
SUBSTEPS = 4
DIRS = 36
FREQ = 16
NX = 32
NY = 512
SX = 16
SY = 256


def touch_ends(values, rng, least, high):
    place = [jax.random.randint(jax.random.fold_in(rng, axis), (), 0, length) for axis, length in enumerate(values.shape)]
    widest = values.shape.index(max(values.shape))
    neighbour = place[:widest] + [(place[widest] + 1) % values.shape[widest]] + place[widest + 1:]
    return values.at[tuple(place)].set(least).at[tuple(neighbour)].set(high)


def steps_of(rng, extent, cuts, smallest, top_value):
    loudness = 1.0
    for position, shards_of in cuts:
        draws = jax.random.uniform(jax.random.fold_in(jax.random.fold_in(rng, 6), position), (shards_of,), jnp.float32, smallest / len(cuts), top_value / len(cuts))
        loudness = loudness * jnp.repeat(jnp.exp(draws), extent[position] // shards_of).reshape((-1,) + (1,) * (len(extent) - 1 - position))
    return loudness


def noise(stream_key, shape, scale, reach, dtype=jnp.bfloat16):
    return jnp.clip(scale * jax.random.normal(stream_key, shape, jnp.float32), -reach, reach).astype(dtype)


def setup_inputs(seed: int = 0, part: int = 0) -> dict:
    streams_of = jax.random.split(jax.random.key(seed), 12)
    part_keys = jax.random.split(jax.random.fold_in(streams_of[11], part), 12)
    return {
        "floc_conc": jnp.clip(jnp.exp(math.log(2.0) - 3.6888794 * jax.random.uniform(part_keys[0], (CLASSES, LEVELS, NX, NY), jnp.float32) ** steps_of(part_keys[0], (CLASSES, LEVELS, NX, NY), ((2, 8), (3, 2)), -0.2, 0.2)), 0.05, 2.0),
        "currents": jnp.clip(jax.random.uniform(part_keys[1], (2, NX, NY), jnp.float32, -0.3, 0.3) * steps_of(part_keys[1], (2, NX, NY), ((1, 8), (2, 2)), -0.4, 0.0), -0.3, 0.3),
        "water_depth": jnp.clip(jnp.exp(math.log(8.0) - 2.7725887 * jax.random.uniform(part_keys[2], (NX, NY), jnp.float32) ** steps_of(part_keys[2], (NX, NY), ((0, 8), (1, 2)), -0.2, 0.2)), 0.5, 8.0),
        "wet_mask": touch_ends((jax.random.randint(part_keys[3], (NX, NY), 0, 10) < 9).astype(jnp.int32), jax.random.fold_in(part_keys[3], 1), 0, 1),
        "shear_rate": jnp.clip(jnp.exp(math.log(1.0) - 2.3025851 * jax.random.uniform(part_keys[4], (LEVELS, NX, NY), jnp.float32) ** steps_of(part_keys[4], (LEVELS, NX, NY), ((1, 8), (2, 2)), -0.2, 0.2)), 0.1, 1.0),
        "aggregation": noise(streams_of[5], (CLASSES, CLASSES), CLASSES ** -0.5, 1.5, jnp.float32),
        "breakup": noise(streams_of[6], (CLASSES, CLASSES), CLASSES ** -0.5, 1.5, jnp.float32),
        "settling": jnp.clip(jnp.exp(jax.random.uniform(streams_of[7], (CLASSES,), jnp.float32, math.log(0.05), math.log(0.4))), 0.05, 0.4),
        "erosion": jnp.clip(jnp.exp(jax.random.uniform(streams_of[8], (CLASSES,), jnp.float32, math.log(0.05), math.log(0.5))), 0.05, 0.5),
        "action_density": jnp.clip(jnp.exp(math.log(2.0) - 2.9957323 * jax.random.uniform(part_keys[9], (DIRS, FREQ, SX, SY), jnp.float32) ** steps_of(part_keys[9], (DIRS, FREQ, SX, SY), ((2, 16),), -0.2, 0.2)), 0.1, 2.0),
        "wind_growth": jnp.clip(jax.random.uniform(streams_of[10], (DIRS, FREQ), jnp.float32, -0.3, 0.3), -0.3, 0.3),
    }


diffusion_rate = 0.05
threshold_stress = 0.25


def coarsen(field):
    row_count, col_count = field.shape
    blocks = field.reshape(row_count // 2, 2, col_count // 2, 2)
    return jnp.sum(blocks, axis=(1, 3)) * 0.25


def shoaling(depth_coarse, freq_count):
    factors = (1.0 + 3.0 * jnp.arange(freq_count).astype(jnp.float32) / freq_count) * 0.25
    return jnp.tanh(depth_coarse[None] * factors[:, None, None])


def stress_excess(eastward, northward, orbital_tile, wet_float):
    orbital_fine = jnp.repeat(jnp.repeat(orbital_tile, 2, axis=0), 2, axis=1)
    stress = 0.5 * (eastward * eastward + northward * northward) + orbital_fine
    return wet_float * jnp.maximum(stress - threshold_stress, 0.0)


def advance(padded, east_padded, north_padded, shear_rate, excess, aggregation, breakup, settling, erosion):
    centre = padded[:, :, 1:-1, 1:-1]
    eastward = east_padded[1:-1, 1:-1]
    northward = north_padded[1:-1, 1:-1]
    give_east = jnp.maximum(east_padded, 0.0) + diffusion_rate
    give_west = jnp.maximum(-east_padded, 0.0) + diffusion_rate
    give_north = jnp.maximum(north_padded, 0.0) + diffusion_rate
    give_south = jnp.maximum(-north_padded, 0.0) + diffusion_rate
    leaving = jnp.abs(eastward) + jnp.abs(northward) + 4.0 * diffusion_rate
    moved_conc = centre - leaving * centre
    moved_conc = moved_conc + give_east[:-2, 1:-1] * padded[:, :, :-2, 1:-1]
    moved_conc = moved_conc + give_west[2:, 1:-1] * padded[:, :, 2:, 1:-1]
    moved_conc = moved_conc + give_north[1:-1, :-2] * padded[:, :, 1:-1, :-2]
    moved_conc = moved_conc + give_south[1:-1, 2:] * padded[:, :, 1:-1, 2:]
    mixed_conc = jnp.einsum("kc,clxy->klxy", aggregation, moved_conc, precision=lax.Precision.HIGHEST)
    broken_up = jnp.einsum("kc,clxy->klxy", breakup, moved_conc, precision=lax.Precision.HIGHEST)
    reacted = moved_conc + 0.25 * shear_rate[None] * moved_conc * mixed_conc + 0.25 * broken_up
    settle_rate = settling[:, None, None, None]
    from_above = jnp.concatenate([reacted[:, 1:], jnp.zeros_like(reacted[:, :1])], axis=1)
    settled = reacted - settle_rate * reacted + settle_rate * from_above
    lifted = erosion[:, None, None] * excess[None]
    return settled.at[:, 0].add(lifted)


def wave_speeds(shoaling_factor, wet_coarse, dir_count):
    angles = (jnp.arange(dir_count).astype(jnp.float32) + 0.5) * (2.0 * math.pi / dir_count) - 0.5 * math.pi
    group_speed = 0.45 * shoaling_factor * wet_coarse[None]
    speed_x = jnp.cos(angles)[:, None, None, None] * group_speed[None]
    speed_y = jnp.sin(angles)[:, None, None, None] * group_speed[None]
    return speed_x, speed_y


def finish_waves(action_density, flux_x, inflow_x, speed_y, shoaling_factor, wind_growth):
    give_north = jnp.maximum(speed_y, 0.0) * action_density
    give_south = jnp.maximum(-speed_y, 0.0) * action_density
    zeros_edge = jnp.zeros_like(action_density[..., :1])
    inflow_y = jnp.concatenate([zeros_edge, give_north[..., :-1]], axis=-1) + jnp.concatenate([give_south[..., 1:], zeros_edge], axis=-1)
    propagated = action_density - flux_x - (give_north + give_south) + inflow_x + inflow_y
    turning = 0.2 * (1.0 - shoaling_factor)[None]
    spread = propagated + turning * (jnp.roll(propagated, 1, axis=0) + jnp.roll(propagated, -1, axis=0) - 2.0 * propagated)
    energy = jnp.mean(spread, axis=(0, 1))
    return spread * jnp.exp(wind_growth[:, :, None, None] - 0.5 * energy[None, None])


def reference(floc_conc, currents, water_depth, wet_mask, shear_rate, aggregation, breakup, settling, erosion, action_density, wind_growth):
    wet_float = wet_mask.astype(jnp.float32)
    eastward = currents[0] * wet_float
    northward = currents[1] * wet_float
    depth_coarse = coarsen(water_depth)
    wet_coarse = coarsen(wet_float)
    shoaling_factor = shoaling(depth_coarse, FREQ)
    orbital = wet_coarse * jnp.mean(action_density * (1.0 - shoaling_factor * shoaling_factor)[None], axis=(0, 1))
    excess = stress_excess(eastward, northward, orbital, wet_float)
    east_padded = jnp.pad(eastward, 1)
    north_padded = jnp.pad(northward, 1)
    floc_state = floc_conc
    for substep in range(SUBSTEPS):
        padded = jnp.pad(floc_state, ((0, 0), (0, 0), (1, 1), (1, 1)))
        floc_state = advance(padded, east_padded, north_padded, shear_rate, excess, aggregation, breakup, settling, erosion)
    speed_x, speed_y = wave_speeds(shoaling_factor, wet_coarse, DIRS)
    flux_x = jnp.abs(speed_x) * action_density
    halfway = DIRS // 2
    zeros_edge = jnp.zeros_like(flux_x[:, :, :1])
    from_west = jnp.concatenate([zeros_edge, flux_x[:, :, :-1]], axis=2)
    from_east = jnp.concatenate([flux_x[:, :, 1:], zeros_edge], axis=2)
    inflow_x = jnp.concatenate([from_west[:halfway], from_east[halfway:]], axis=0)
    action_next = finish_waves(action_density, flux_x, inflow_x, speed_y, shoaling_factor, wind_growth)
    return floc_state, action_next
```

```python
import functools
import math

import jax
import jax.numpy as jnp
import numpy as np
from jax import lax
from jax.experimental import pallas as pl
from jax.experimental.pallas import tpu as pltpu
from jax.sharding import PartitionSpec as P

SUBSTEPS = 4
GROUPS = 4
diffusion_rate = 0.05
threshold_stress = 0.25
MESH = pl.DeviceIdType.MESH
HIGHEST = lax.Precision.HIGHEST


def roll(x, shift, axis):
    shift = shift % x.shape[axis]
    return x if shift == 0 else pltpu.roll(x, shift, axis)


def iota(shape, dim):
    return lax.broadcasted_iota(jnp.int32, shape, dim)


def kernel(
    classes,
    levels,
    dirs,
    freqs,
    pairs,
    floc_ref,
    cur_ref,
    depth_ref,
    wet_ref,
    shear_ref,
    agg_ref,
    brk_ref,
    settling_ref,
    erosion_ref,
    act_ref,
    wind_ref,
    trig_ref,
    floc_out,
    act_out,
    conc,
    shear,
    coef,
    excess,
    above,
    moved,
    init_send,
    init_recv,
    row_send,
    row_recv,
    col_send,
    col_recv,
    back_send,
    back_recv,
    small_send,
    small_recv,
    flux_send,
    flux_recv,
    prop,
    fields,
    init_sems,
    edge_sems,
    back_sems,
    small_sems,
    flux_sems,
):
    along = lax.axis_index("along")
    core = lax.axis_index("cross")
    x = along % 2
    z = along // 2
    own_half = (x + core) % 2
    per = levels // GROUPS
    layers = classes * per
    sub = iota((8, 128), 0)
    lane = iota((8, 128), 1)
    low = sub < 4

    def same(scalar, value):
        return jnp.full((8, 128), scalar, jnp.int32) == value

    core1 = same(core, 1)
    x1 = same(x, 1)
    pair_id = {"along": along + 1 - 2 * x}
    core_id = {"cross": 1 - core}
    place = x + core * (3 - 2 * x)
    outer_wave = jnp.where(core == 1, along + 1, along - 1)
    has_outer = (outer_wave >= 0) & (outer_wave < 2 * pairs)
    outer_id = {"along": outer_wave, "cross": 1 - core}
    has_low = z > 0
    has_high = z < pairs - 1
    low_id = {"along": along - 2}
    high_id = {"along": along + 2}

    barrier = pltpu.get_barrier_semaphore()
    pl.semaphore_signal(barrier, inc=1, device_id=pair_id, device_id_type=MESH)
    pl.semaphore_signal(barrier, inc=1, device_id=core_id, device_id_type=MESH)

    @pl.when(has_low)
    def _():
        pl.semaphore_signal(barrier, inc=1, device_id=low_id, device_id_type=MESH)

    @pl.when(has_high)
    def _():
        pl.semaphore_signal(barrier, inc=1, device_id=high_id, device_id_type=MESH)

    @pl.when(has_outer)
    def _():
        pl.semaphore_signal(barrier, inc=1, device_id=outer_id, device_id_type=MESH)

    wet = wet_ref[...].astype(jnp.float32)
    east_tile = cur_ref[0] * wet
    north_tile = cur_ref[1] * wet
    depth = depth_ref[...]

    def pack_pair(first, second, take_high):
        return jnp.where(
            take_high,
            jnp.where(low, pltpu.roll(first, 4, 0), second),
            jnp.where(low, first, pltpu.roll(second, 4, 0)),
        )

    send_high = same(own_half, 0)

    def fill(group):
        for k in range(classes):
            init_send[group, pl.ds(8 * k, 8)] = pack_pair(
                floc_ref[k, levels - 1 - 2 * group], floc_ref[k, levels - 2 - 2 * group], send_high
            )
        init_send[group, pl.ds(8 * classes, 8)] = pack_pair(east_tile, north_tile, send_high)
        init_send[group, pl.ds(8 * classes + 8, 8)] = pack_pair(
            shear_ref[levels - 1 - 2 * group], shear_ref[levels - 2 - 2 * group], send_high
        )

    def init_copy(group):
        return pltpu.make_async_remote_copy(
            src_ref=init_send.at[group],
            dst_ref=init_recv.at[group],
            send_sem=init_sems.at[0, group],
            recv_sem=init_sems.at[1, group],
            device_id=pair_id,
            device_id_type=MESH,
        )

    def back_copy(group):
        return pltpu.make_async_remote_copy(
            src_ref=back_send.at[group],
            dst_ref=back_recv.at[group],
            send_sem=back_sems.at[0, group],
            recv_sem=back_sems.at[1, group],
            device_id=pair_id,
            device_id_type=MESH,
        )

    def small_copy(slot, target):
        return pltpu.make_async_remote_copy(
            src_ref=small_send.at[slot],
            dst_ref=small_recv.at[slot],
            send_sem=small_sems.at[0, slot],
            recv_sem=small_sems.at[1, slot],
            device_id=target,
            device_id_type=MESH,
        )

    def row_copy(slot, side, target):
        return pltpu.make_async_remote_copy(
            src_ref=row_send.at[slot, side],
            dst_ref=row_recv.at[slot, side],
            send_sem=edge_sems.at[0, slot, side],
            recv_sem=edge_sems.at[1, slot, side],
            device_id=target,
            device_id_type=MESH,
        )

    def col_copy(slot, side, target):
        return pltpu.make_async_remote_copy(
            src_ref=col_send.at[slot, side],
            dst_ref=col_recv.at[slot, side],
            send_sem=edge_sems.at[0, slot, 2 + side],
            recv_sem=edge_sems.at[1, slot, 2 + side],
            device_id=target,
            device_id_type=MESH,
        )

    up_is_pair = (place == 0) | (place == 2)
    down_is_pair = (place == 1) | (place == 3)
    pair_along = along + 1 - 2 * x
    up_id = {
        "along": jnp.where(up_is_pair, pair_along, along),
        "cross": jnp.where(up_is_pair, core, 1 - core),
    }
    down_id = {
        "along": jnp.where(down_is_pair, pair_along, along),
        "cross": jnp.where(down_is_pair, core, 1 - core),
    }
    has_up = place < 3
    has_down = place > 0

    edges = (
        (has_high, functools.partial(row_copy, side=0, target=high_id)),
        (has_low, functools.partial(row_copy, side=1, target=low_id)),
        (has_up, functools.partial(col_copy, side=0, target=up_id)),
        (has_down, functools.partial(col_copy, side=1, target=down_id)),
    )
    arrives = (has_low, has_high, has_down, has_up)

    lax.fori_loop(0, GROUPS, lambda g, c: (fill(g), c)[1], 0)

    a_in = iota((128, 128), 0)
    b_in = iota((128, 128), 1)
    gather = [jnp.where(a_in // 2 + 64 * j == b_in, 0.25, 0.0).astype(jnp.float32) for j in range(2)]
    spreadm = [jnp.where(a_in == 64 * j + b_in // 2, 1.0, 0.0).astype(jnp.float32) for j in range(2)]

    def coarse(v):
        v = v + pltpu.roll(v, 7, 0)
        c0 = jnp.dot(v, gather[0], precision=HIGHEST, preferred_element_type=jnp.float32)
        c1 = jnp.dot(v, gather[1], precision=HIGHEST, preferred_element_type=jnp.float32)
        return c0 + pltpu.roll(c1, 4, 0)

    depth_c = coarse(depth)
    wet_c = coarse(wet)
    both = jnp.where(sub % 2 == 0, depth_c, pltpu.roll(wet_c, 1, 0))
    mine_c = jnp.where(core1, pltpu.roll(both, 6, 0), both)
    small_send[0] = jnp.where(core1, both, pltpu.roll(both, 6, 0))

    for side, here in enumerate(arrives):

        @pl.when(jnp.logical_not(here))
        def _(side=side):
            def clear(slot, carry):
                if side < 2:
                    row_recv[slot, side] = jnp.zeros((32, 128), jnp.float32)
                else:
                    col_recv[slot, side - 2] = jnp.zeros((8, 128), jnp.float32)
                return carry

            lax.fori_loop(0, SUBSTEPS * GROUPS, clear, 0)

    half_rows = flux_recv.shape[0] // 2
    block = 2 * freqs

    @pl.when(jnp.logical_not(has_outer))
    def _():
        def clear(d, carry):
            start = pl.multiple_of(core * half_rows + d * block, 8)
            flux_recv[pl.ds(start, block)] = jnp.zeros((block, 128), jnp.float32)
            return carry

        lax.fori_loop(0, dirs // 2, clear, 0)

    above[...] = jnp.zeros_like(above)
    excess[...] = jnp.zeros_like(excess)

    waits = 2 + has_low.astype(jnp.int32) + has_high.astype(jnp.int32) + has_outer.astype(jnp.int32)
    pl.semaphore_wait(barrier, waits)
    small_copy(0, core_id).start()
    for g in range(GROUPS):
        init_copy(g).start()

    def add_dir(d, acc):
        return acc + act_ref[pl.ds(pl.multiple_of(d * block, 8), block)]

    total = lax.fori_loop(0, dirs, add_dir, jnp.zeros((block, 128), jnp.float32), unroll=4)

    small_copy(0, core_id).wait_recv()
    other_c = small_recv[0]
    first = jnp.where(core1, other_c, mine_c)
    second = jnp.where(core1, mine_c, other_c)
    even = iota((block, 128), 0) % 2 == 0

    def rows_of(row):
        return jnp.where(
            even,
            jnp.broadcast_to(first[row : row + 1], (block, 128)),
            jnp.broadcast_to(second[row : row + 1], (block, 128)),
        )

    depth_w = rows_of(0)
    wet_w = rows_of(1)
    freq = (iota((block, 128), 0) // 2).astype(jnp.float32)
    shoal = jnp.tanh(depth_w * ((1.0 + 3.0 * freq / freqs) * 0.25))
    speed = 0.45 * shoal * wet_w
    fields[0] = speed
    fields[1] = 0.2 * (1.0 - shoal)

    def sum_rows(v):
        v8 = v[0:8]
        for i in range(1, block // 8):
            v8 = v8 + v[8 * i : 8 * i + 8]
        v8 = v8 + pltpu.roll(v8, 4, 0)
        return v8 + pltpu.roll(v8, 2, 0)

    scale = 1.0 / (dirs * freqs)
    orbital = wet_w[0:8] * (sum_rows(total * (1.0 - shoal * shoal)) * scale)
    flip = pltpu.roll(orbital, 1, 0)
    small_send[1] = jnp.where(core1, orbital, flip)
    small_copy(1, core_id).start()
    mine_o = jnp.where(core1, flip, orbital)

    def flux(d, carry):
        start = pl.multiple_of(d * block, 8)
        flux_send[pl.ds(start, block)] = (trig_ref[0, d] * fields[0]) * act_ref[pl.ds(start, block)]
        return carry

    lax.fori_loop(0, dirs, flux, 0, unroll=2)

    def flux_copy(side, target):
        part = pl.ds(side * half_rows, half_rows)
        return pltpu.make_async_remote_copy(
            src_ref=flux_send.at[part],
            dst_ref=flux_recv.at[part],
            send_sem=flux_sems.at[0, side],
            recv_sem=flux_sems.at[1, side],
            device_id=target,
            device_id_type=MESH,
        )

    @pl.when(core == 0)
    def _():
        flux_copy(0, core_id).start()

    @pl.when(core == 1)
    def _():
        flux_copy(1, core_id).start()

    @pl.when((core == 1) & has_outer)
    def _():
        flux_copy(0, outer_id).start()

    @pl.when((core == 0) & has_outer)
    def _():
        flux_copy(1, outer_id).start()

    small_copy(1, core_id).wait_recv()
    other_o = small_recv[1]
    coarse0 = jnp.where(core1, other_o, mine_o)[0:1]
    coarse1 = jnp.where(core1, mine_o, other_o)[0:1]
    tall = jnp.where(
        sub % 4 < 2, jnp.broadcast_to(coarse0, (8, 128)), jnp.broadcast_to(coarse1, (8, 128))
    )
    fine = jnp.where(
        low,
        jnp.dot(tall, spreadm[0], precision=HIGHEST, preferred_element_type=jnp.float32),
        jnp.dot(tall, spreadm[1], precision=HIGHEST, preferred_element_type=jnp.float32),
    )
    stress = 0.5 * (east_tile * east_tile + north_tile * north_tile) + fine
    excess_tile = wet * jnp.maximum(stress - threshold_stress, 0.0)
    small_send[2] = pack_pair(excess_tile, excess_tile, send_high)
    small_copy(2, pair_id).start()

    my_rows = sub // 4 == jnp.full((8, 128), x, jnp.int32)

    def place_own(v):
        return jnp.where(core1, pltpu.roll(v, 4, 0), v)

    def unpack_pair(first, second, packed):
        turned = pltpu.roll(packed, 4, 0)
        return (
            jnp.where(my_rows, place_own(first), jnp.where(x1, packed, turned)),
            jnp.where(my_rows, place_own(second), jnp.where(x1, turned, packed)),
        )

    def send_edges(group, slot):
        rows = [conc[group, pl.ds(8 * u, 8)] for u in range(layers + 2)]
        row_send[slot, 0] = conc.at[group][pl.ds(7, 32, stride=8), :]
        row_send[slot, 1] = conc.at[group][pl.ds(0, 32, stride=8), :]
        right = jnp.zeros((8, 128), jnp.float32)
        left = jnp.zeros((8, 128), jnp.float32)
        for u, v in enumerate(rows):
            right = jnp.where(lane == u, roll(v, u + 1, 1), right)
            left = jnp.where(lane == u, roll(v, u, 1), left)
        col_send[slot, 0] = right
        col_send[slot, 1] = left
        for here, copy in edges:

            @pl.when(here)
            def _(copy=copy):
                copy(slot).start()

    def begin(group):
        init_copy(group).wait_recv()
        for k in range(classes):
            t0, t1 = unpack_pair(
                floc_ref[k, levels - 1 - 2 * group],
                floc_ref[k, levels - 2 - 2 * group],
                init_recv[group, pl.ds(8 * k, 8)],
            )
            conc[group, pl.ds(16 * k, 8)] = t0
            conc[group, pl.ds(16 * k + 8, 8)] = t1
        e, n = unpack_pair(east_tile, north_tile, init_recv[group, pl.ds(8 * classes, 8)])
        conc[group, pl.ds(8 * layers, 8)] = e
        conc[group, pl.ds(8 * layers + 8, 8)] = n
        s0, s1 = unpack_pair(
            shear_ref[levels - 1 - 2 * group],
            shear_ref[levels - 2 - 2 * group],
            init_recv[group, pl.ds(8 * classes + 8, 8)],
        )
        shear[group, 0] = 0.25 * s0
        shear[group, 1] = 0.25 * s1
        send_edges(group, group)

    begin(0)

    top = sub == 0
    bottom = sub == 7
    first_lane = lane == 0
    last_lane = lane == 127

    def step(t, carry):
        s = t // GROUPS
        g = t % GROUPS

        @pl.when(t < GROUPS - 1)
        def _():
            begin(g + 1)

        for side, (here, (_, copy)) in enumerate(zip(arrives, edges)):

            @pl.when(here)
            def _(copy=copy):
                copy(t).wait_recv()

        from_low = row_recv.at[t, 0]
        from_high = row_recv.at[t, 1]
        from_left = col_recv[t, 0]
        from_right = col_recv[t, 1]

        def neighbours(u, v):
            west = jnp.where(top, from_low[pl.ds(u, 1)], pltpu.roll(v, 1, 0))
            east = jnp.where(bottom, from_high[pl.ds(u, 1)], pltpu.roll(v, 7, 0))
            south = jnp.where(first_lane, roll(from_left, 128 - u, 1), pltpu.roll(v, 1, 1))
            north = jnp.where(last_lane, roll(from_right, 127 - u, 1), pltpu.roll(v, 127, 1))
            return west, east, south, north

        @pl.when(t == 0)
        def _():
            e = conc[0, pl.ds(8 * layers, 8)]
            n = conc[0, pl.ds(8 * layers + 8, 8)]
            e_w, e_e, _, _ = neighbours(layers, e)
            _, _, n_s, n_n = neighbours(layers + 1, n)
            zero = jnp.zeros((8, 128), jnp.float32)

            def rate(v, edge, here):
                give = jnp.maximum(v, 0.0) + diffusion_rate
                return jnp.where(edge & same(here.astype(jnp.int32), 0), zero, give)

            coef[0] = 1.0 - (jnp.abs(e) + jnp.abs(n) + 4.0 * diffusion_rate)
            coef[1] = rate(e_w, top, has_low)
            coef[2] = rate(-e_e, bottom, has_high)
            coef[3] = rate(n_s, first_lane, has_down)
            coef[4] = rate(-n_n, last_lane, has_up)

        @pl.when(t == GROUPS - 1)
        def _():
            small_copy(2, pair_id).wait_recv()
            ex, _ = unpack_pair(excess_tile, excess_tile, small_recv[2])
            excess[...] = ex

        keep, c_w, c_e, c_s, c_n = [coef[i] for i in range(5)]
        for u in range(layers):
            v = conc[g, pl.ds(8 * u, 8)]
            west, east, south, north = neighbours(u, v)
            moved[pl.ds(8 * u, 8)] = (
                keep * v + (c_w * west + c_e * east) + (c_s * south + c_n * north)
            )
        sh = [shear[g, 0], shear[g, 1]]
        last_group = same(g, GROUPS - 1)
        ex = jnp.where(last_group, excess[...], 0.0)
        mv = [moved[pl.ds(8 * u, 8)] for u in range(layers)]
        for k in range(classes):
            mix = [None, None]
            brk = [None, None]
            for m in range(classes):
                a = agg_ref[k, m]
                b = brk_ref[k, m]
                for p in range(2):
                    v = mv[2 * m + p]
                    mix[p] = a * v if m == 0 else mix[p] + a * v
                    brk[p] = b * v if m == 0 else brk[p] + b * v
            r = [
                mv[2 * k + p] + sh[p] * mv[2 * k + p] * mix[p] + 0.25 * brk[p] for p in range(2)
            ]
            w = settling_ref[k]
            top_above = above[pl.ds(8 * k, 8)]
            conc[g, pl.ds(16 * k, 8)] = r[0] - w * r[0] + w * top_above
            conc[g, pl.ds(16 * k + 8, 8)] = r[1] - w * r[1] + w * r[0] + erosion_ref[k] * ex
            above[pl.ds(8 * k, 8)] = jnp.where(last_group, 0.0, r[1])

        @pl.when(s < SUBSTEPS - 1)
        def _():
            send_edges(g, t + GROUPS)

        @pl.when(s == SUBSTEPS - 1)
        def _():
            for k in range(classes):
                back_send[g, pl.ds(8 * k, 8)] = pack_pair(
                    conc[g, pl.ds(16 * k, 8)], conc[g, pl.ds(16 * k + 8, 8)], same(x, 0)
                )
            back_copy(g).start()

        return carry

    lax.fori_loop(0, SUBSTEPS * GROUPS, step, 0)

    @pl.when((core == 1) | has_outer)
    def _():
        flux_copy(0, core_id).wait_recv()

    @pl.when((core == 0) | has_outer)
    def _():
        flux_copy(1, core_id).wait_recv()

    wide_lane = iota((block, 128), 1)

    def propagate(northward, d, acc):
        start = pl.multiple_of(d * block, 8)
        a = act_ref[pl.ds(start, block)]
        give = (trig_ref[1, d] * fields[0]) * a
        if northward:
            r = pltpu.roll(give, 1, 1)
            fix = jnp.where(even, 0.0, pltpu.roll(r, 1, 0))
            inflow = jnp.where(wide_lane == 0, fix, r)
        else:
            r = pltpu.roll(give, 127, 1)
            fix = jnp.where(even, pltpu.roll(r, block - 1, 0), 0.0)
            inflow = jnp.where(wide_lane == 127, fix, r)
        p = a - flux_send[pl.ds(start, block)] - give + flux_recv[pl.ds(start, block)] + inflow
        prop[pl.ds(start, block)] = p
        return acc + p

    quarter = dirs // 4
    acc = jnp.zeros((block, 128), jnp.float32)
    acc = lax.fori_loop(0, quarter, functools.partial(propagate, False), acc)
    acc = lax.fori_loop(quarter, 3 * quarter, functools.partial(propagate, True), acc)
    acc = lax.fori_loop(3 * quarter, dirs, functools.partial(propagate, False), acc)
    decay = jnp.exp(-0.5 * (sum_rows(acc) * scale))
    decay = jnp.concatenate([decay] * (block // 8), axis=0)
    grow = jnp.exp(wind_ref[...])
    pick = jnp.where(iota((block, freqs), 0) // 2 == iota((block, freqs), 1), 1.0, 0.0)
    grow = jnp.dot(
        pick.astype(jnp.float32), grow, precision=HIGHEST, preferred_element_type=jnp.float32
    )
    turning = fields[1]

    def finish(d, g):
        before = jnp.where(d == 0, dirs - 1, d - 1)
        after = jnp.where(d == dirs - 1, 0, d + 1)
        p = prop[pl.ds(pl.multiple_of(d * block, 8), block)]
        pb = prop[pl.ds(pl.multiple_of(before * block, 8), block)]
        pa = prop[pl.ds(pl.multiple_of(after * block, 8), block)]
        spread = p + turning * (pb + pa - 2.0 * p)
        factor = jnp.broadcast_to(g[:, 0:1], (block, 128)) * decay
        act_out[pl.ds(pl.multiple_of(d * block, 8), block)] = spread * factor
        return pltpu.roll(g, 127, 1)

    lax.fori_loop(0, dirs, finish, grow)

    own = sub // 4 == jnp.full((8, 128), own_half, jnp.int32)
    own1 = same(own_half, 1)

    def gather_back(g, carry):
        back_copy(g).wait_recv()
        for k in range(classes):
            packed = back_recv[g, pl.ds(8 * k, 8)]
            turned = pltpu.roll(packed, 4, 0)
            t0 = place_own(conc[g, pl.ds(16 * k, 8)])
            t1 = place_own(conc[g, pl.ds(16 * k + 8, 8)])
            floc_out[k, levels - 1 - 2 * g] = jnp.where(
                own, t0, jnp.where(own1, packed, turned)
            )
            floc_out[k, levels - 2 - 2 * g] = jnp.where(
                own, t1, jnp.where(own1, turned, packed)
            )
        return carry

    lax.fori_loop(0, GROUPS, gather_back, 0)

    small_copy(0, core_id).wait_send()
    small_copy(1, core_id).wait_send()
    small_copy(2, pair_id).wait_send()

    def drain_groups(g, carry):
        init_copy(g).wait_send()
        back_copy(g).wait_send()
        return carry

    lax.fori_loop(0, GROUPS, drain_groups, 0)

    def drain_edges(t, carry):
        for here, copy in edges:

            @pl.when(here)
            def _(copy=copy):
                copy(t).wait_send()

        return carry

    lax.fori_loop(0, SUBSTEPS * GROUPS, drain_edges, 0)

    @pl.when((core == 0) | has_outer)
    def _():
        flux_copy(0, core_id).wait_send()

    @pl.when((core == 1) | has_outer)
    def _():
        flux_copy(1, core_id).wait_send()


def halves(tile):
    rows = tile.shape[-2]
    split = tile.reshape(tile.shape[:-1] + (2, 128))
    return jnp.swapaxes(split, -3, -2).reshape(tile.shape[:-2] + (2 * rows, 128))


def unhalves(tile):
    rows = tile.shape[-2] // 2
    split = tile.reshape(tile.shape[:-2] + (2, rows, 128))
    return jnp.swapaxes(split, -3, -2).reshape(tile.shape[:-2] + (rows, 256))


def body(
    pairs,
    floc_conc,
    currents,
    water_depth,
    wet_mask,
    shear_rate,
    aggregation,
    breakup,
    settling,
    erosion,
    action_density,
    wind_growth,
):
    classes, levels = floc_conc.shape[:2]
    dirs, freqs = wind_growth.shape
    rows = dirs * freqs * 2
    angles = (np.arange(dirs) + 0.5) * (2.0 * math.pi / dirs) - 0.5 * math.pi
    trig = jnp.asarray(np.abs(np.stack([np.cos(angles), np.sin(angles)])).astype(np.float32))
    wind = jnp.pad(wind_growth.T, ((0, 0), (0, 128 - dirs)))
    vmem = pl.BlockSpec(memory_space=pltpu.VMEM)
    smem = pl.BlockSpec(memory_space=pltpu.SMEM)
    slots = SUBSTEPS * GROUPS
    f32 = jnp.float32
    V = pltpu.VMEM
    out_floc, out_act = pl.pallas_call(
        functools.partial(kernel, classes, levels, dirs, freqs, pairs),
        out_shape=(
            jax.ShapeDtypeStruct((classes, levels, 8, 128), f32),
            jax.ShapeDtypeStruct((rows, 128), f32),
        ),
        in_specs=[vmem] * 5 + [smem] * 4 + [vmem, vmem, smem],
        out_specs=(vmem, vmem),
        scratch_shapes=[
            V((GROUPS, 32 * 8, 128), f32),
            V((GROUPS, 2, 8, 128), f32),
            V((5, 8, 128), f32),
            V((8, 128), f32),
            V((classes * 8, 128), f32),
            V((classes * 16, 128), f32),
            V((GROUPS, classes * 8 + 16, 128), f32),
            V((GROUPS, classes * 8 + 16, 128), f32),
            V((slots, 2, 32, 128), f32),
            V((slots, 2, 32, 128), f32),
            V((slots, 2, 8, 128), f32),
            V((slots, 2, 8, 128), f32),
            V((GROUPS, classes * 8, 128), f32),
            V((GROUPS, classes * 8, 128), f32),
            V((3, 8, 128), f32),
            V((3, 8, 128), f32),
            V((rows, 128), f32),
            V((rows, 128), f32),
            V((rows, 128), f32),
            V((2, 2 * freqs, 128), f32),
            pltpu.SemaphoreType.DMA((2, GROUPS)),
            pltpu.SemaphoreType.DMA((2, slots, 4)),
            pltpu.SemaphoreType.DMA((2, GROUPS)),
            pltpu.SemaphoreType.DMA((2, 3)),
            pltpu.SemaphoreType.DMA((2, 2)),
        ],
        compiler_params=pltpu.CompilerParams(
            collective_id=0, has_side_effects=True, vmem_limit_bytes=32 * 1024 * 1024
        ),
    )(
        halves(floc_conc),
        halves(currents),
        halves(water_depth),
        halves(wet_mask),
        halves(shear_rate),
        aggregation,
        breakup,
        settling,
        erosion,
        action_density.reshape(rows, 128),
        wind,
        trig,
    )
    return unhalves(out_floc), out_act.reshape(action_density.shape)


def solution(mesh):
    placed = (
        P(None, None, ("group", "along"), "cross"),
        P(None, ("group", "along"), "cross"),
        P(("group", "along"), "cross"),
        P(("group", "along"), "cross"),
        P(None, ("group", "along"), "cross"),
        P(),
        P(),
        P(),
        P(),
        P(None, None, ("group", "along", "cross"), None),
        P(),
    )
    return jax.shard_map(
        functools.partial(body, mesh.shape["along"] // 2),
        mesh=mesh,
        in_specs=placed,
        out_specs=(
            P(None, None, ("group", "along"), "cross"),
            P(None, None, ("group", "along", "cross"), None),
        ),
        check_vma=False,
    )
```

```python
import functools
import math

import jax
import jax.numpy as jnp
import numpy as np
from jax import lax
from jax.experimental import pallas as pl
from jax.experimental.pallas import tpu as pltpu
from jax.sharding import PartitionSpec as P

SUBSTEPS = 4
GROUPS = 4
CHUNKS = 8
diffusion_rate = 0.05
threshold_stress = 0.25
MESH = pl.DeviceIdType.MESH
HIGHEST = lax.Precision.HIGHEST


def roll(x, shift, axis):
    shift = shift % x.shape[axis]
    return x if shift == 0 else pltpu.roll(x, shift, axis)


def iota(shape, dim):
    return lax.broadcasted_iota(jnp.int32, shape, dim)


def kernel(
    classes,
    levels,
    dirs,
    freqs,
    pairs,
    floc_hbm,
    cur_hbm,
    depth_hbm,
    wet_hbm,
    shear_hbm,
    agg_hbm,
    brk_hbm,
    settling_hbm,
    erosion_hbm,
    act_hbm,
    wind_hbm,
    trig_hbm,
    floc_out,
    act_out,
    conc,
    shear,
    coef,
    excess,
    above,
    moved,
    init_send,
    init_recv,
    row_send,
    row_recv,
    col_send,
    col_recv,
    back_send,
    back_recv,
    small_send,
    small_recv,
    flux_send,
    flux_recv,
    prop,
    fields,
    growth,
    wave_sum,
    decay_ref,
    floc_ref,
    cur_ref,
    depth_ref,
    wet_ref,
    shear_ref,
    agg_ref,
    brk_ref,
    settling_ref,
    erosion_ref,
    act_ref,
    wind_ref,
    trig_ref,
    load_sems,
    init_sems,
    edge_sems,
    back_sems,
    small_sems,
    flux_sems,
):
    along = lax.axis_index("along")
    core = lax.axis_index("cross")
    x = along % 2
    z = along // 2
    own_half = (x + core) % 2
    per = levels // GROUPS
    layers = classes * per
    sub = iota((8, 128), 0)
    lane = iota((8, 128), 1)
    low = sub < 4

    def same(scalar, value):
        return jnp.full((8, 128), scalar, jnp.int32) == value

    core1 = same(core, 1)
    x1 = same(x, 1)
    pair_id = {"along": along + 1 - 2 * x}
    core_id = {"cross": 1 - core}
    place = x + core * (3 - 2 * x)
    outer_wave = jnp.where(core == 1, along + 1, along - 1)
    has_outer = (outer_wave >= 0) & (outer_wave < 2 * pairs)
    outer_id = {"along": outer_wave, "cross": 1 - core}
    has_low = z > 0
    has_high = z < pairs - 1
    low_id = {"along": along - 2}
    high_id = {"along": along + 2}

    loads = [
        pltpu.make_async_copy(src, dst, load_sems.at[i])
        for i, (src, dst) in enumerate(
            (
                (wet_hbm, wet_ref),
                (cur_hbm, cur_ref),
                (depth_hbm, depth_ref),
                (shear_hbm, shear_ref),
                (floc_hbm, floc_ref),
                (act_hbm, act_ref),
                (trig_hbm, trig_ref),
                (agg_hbm, agg_ref),
                (brk_hbm, brk_ref),
                (settling_hbm, settling_ref),
                (erosion_hbm, erosion_ref),
                (wind_hbm, wind_ref),
            )
        )
    ]
    barrier = pltpu.get_barrier_semaphore()
    pl.semaphore_signal(barrier, inc=1, device_id=pair_id, device_id_type=MESH)
    pl.semaphore_signal(barrier, inc=1, device_id=core_id, device_id_type=MESH)

    @pl.when(has_low)
    def _():
        pl.semaphore_signal(barrier, inc=1, device_id=low_id, device_id_type=MESH)

    @pl.when(has_high)
    def _():
        pl.semaphore_signal(barrier, inc=1, device_id=high_id, device_id_type=MESH)

    @pl.when(has_outer)
    def _():
        pl.semaphore_signal(barrier, inc=1, device_id=outer_id, device_id_type=MESH)

    for load in loads:
        load.start()
    for load in loads[:4]:
        load.wait()

    wet = wet_ref[...].astype(jnp.float32)
    east_tile = cur_ref[0] * wet
    north_tile = cur_ref[1] * wet
    depth = depth_ref[...]

    def pack_pair(first, second, take_high):
        return jnp.where(
            take_high,
            jnp.where(low, pltpu.roll(first, 4, 0), second),
            jnp.where(low, first, pltpu.roll(second, 4, 0)),
        )

    send_high = same(own_half, 0)

    def fill(group):
        for k in range(classes):
            init_send[group, pl.ds(8 * k, 8)] = pack_pair(
                floc_ref[k, levels - 1 - 2 * group], floc_ref[k, levels - 2 - 2 * group], send_high
            )
        init_send[group, pl.ds(8 * classes, 8)] = pack_pair(east_tile, north_tile, send_high)
        init_send[group, pl.ds(8 * classes + 8, 8)] = pack_pair(
            shear_ref[levels - 1 - 2 * group], shear_ref[levels - 2 - 2 * group], send_high
        )

    def init_copy(group):
        return pltpu.make_async_remote_copy(
            src_ref=init_send.at[group],
            dst_ref=init_recv.at[group],
            send_sem=init_sems.at[0, group],
            recv_sem=init_sems.at[1, group],
            device_id=pair_id,
            device_id_type=MESH,
        )

    def back_copy(group):
        return pltpu.make_async_remote_copy(
            src_ref=back_send.at[group],
            dst_ref=back_recv.at[group],
            send_sem=back_sems.at[0, group],
            recv_sem=back_sems.at[1, group],
            device_id=pair_id,
            device_id_type=MESH,
        )

    def small_copy(slot, target):
        return pltpu.make_async_remote_copy(
            src_ref=small_send.at[slot],
            dst_ref=small_recv.at[slot],
            send_sem=small_sems.at[0, slot],
            recv_sem=small_sems.at[1, slot],
            device_id=target,
            device_id_type=MESH,
        )

    def row_copy(slot, side, target):
        return pltpu.make_async_remote_copy(
            src_ref=row_send.at[slot, side],
            dst_ref=row_recv.at[slot, side],
            send_sem=edge_sems.at[0, slot, side],
            recv_sem=edge_sems.at[1, slot, side],
            device_id=target,
            device_id_type=MESH,
        )

    def col_copy(slot, side, target):
        return pltpu.make_async_remote_copy(
            src_ref=col_send.at[slot, side],
            dst_ref=col_recv.at[slot, side],
            send_sem=edge_sems.at[0, slot, 2 + side],
            recv_sem=edge_sems.at[1, slot, 2 + side],
            device_id=target,
            device_id_type=MESH,
        )

    up_is_pair = (place == 0) | (place == 2)
    down_is_pair = (place == 1) | (place == 3)
    pair_along = along + 1 - 2 * x
    up_id = {
        "along": jnp.where(up_is_pair, pair_along, along),
        "cross": jnp.where(up_is_pair, core, 1 - core),
    }
    down_id = {
        "along": jnp.where(down_is_pair, pair_along, along),
        "cross": jnp.where(down_is_pair, core, 1 - core),
    }
    has_up = place < 3
    has_down = place > 0

    edges = (
        (has_high, functools.partial(row_copy, side=0, target=high_id)),
        (has_low, functools.partial(row_copy, side=1, target=low_id)),
        (has_up, functools.partial(col_copy, side=0, target=up_id)),
        (has_down, functools.partial(col_copy, side=1, target=down_id)),
    )
    arrives = (has_low, has_high, has_down, has_up)

    a_in = iota((128, 128), 0)
    b_in = iota((128, 128), 1)
    gather = [jnp.where(a_in // 2 + 64 * j == b_in, 0.25, 0.0).astype(jnp.float32) for j in range(2)]
    spreadm = [jnp.where(a_in == 64 * j + b_in // 2, 1.0, 0.0).astype(jnp.float32) for j in range(2)]

    def coarse(v):
        v = v + pltpu.roll(v, 7, 0)
        c0 = jnp.dot(v, gather[0], precision=HIGHEST, preferred_element_type=jnp.float32)
        c1 = jnp.dot(v, gather[1], precision=HIGHEST, preferred_element_type=jnp.float32)
        return c0 + pltpu.roll(c1, 4, 0)

    depth_c = coarse(depth)
    wet_c = coarse(wet)
    both = jnp.where(sub % 2 == 0, depth_c, pltpu.roll(wet_c, 1, 0))
    mine_c = jnp.where(core1, pltpu.roll(both, 6, 0), both)
    small_send[0] = jnp.where(core1, both, pltpu.roll(both, 6, 0))

    for side, here in enumerate(arrives):

        @pl.when(jnp.logical_not(here))
        def _(side=side):
            def clear(slot, carry):
                if side < 2:
                    row_recv[slot, side] = jnp.zeros((32, 128), jnp.float32)
                else:
                    col_recv[slot, side - 2] = jnp.zeros((8, 128), jnp.float32)
                return carry

            lax.fori_loop(0, SUBSTEPS * GROUPS, clear, 0)

    half_rows = flux_recv.shape[0] // 2
    block = 2 * freqs
    chunk_rows = half_rows // CHUNKS
    flux_goes = ((core == 0) | has_outer, (core == 1) | has_outer)
    flux_comes = ((core == 1) | has_outer, (core == 0) | has_outer)
    flux_along = (
        jnp.where(core == 0, along, along + 1),
        jnp.where(core == 1, along, along - 1),
    )

    def flux_copy(side, chunk):
        start = side * half_rows + chunk * chunk_rows
        part = pl.ds(pl.multiple_of(start, 8), chunk_rows)
        return pltpu.make_async_remote_copy(
            src_ref=flux_send.at[part],
            dst_ref=flux_recv.at[part],
            send_sem=flux_sems.at[0, side, chunk],
            recv_sem=flux_sems.at[1, side, chunk],
            device_id={"along": flux_along[side], "cross": 1 - core},
            device_id_type=MESH,
        )


    @pl.when(jnp.logical_not(has_outer))
    def _():
        def clear(d, carry):
            start = pl.multiple_of(core * half_rows + d * block, 8)
            flux_recv[pl.ds(start, block)] = jnp.zeros((block, 128), jnp.float32)
            return carry

        lax.fori_loop(0, dirs // 2, clear, 0)

    above[...] = jnp.zeros_like(above)
    excess[...] = jnp.zeros_like(excess)

    loads[4].wait()
    fill(0)
    waits = 2 + has_low.astype(jnp.int32) + has_high.astype(jnp.int32) + has_outer.astype(jnp.int32)
    pl.semaphore_wait(barrier, waits)
    small_copy(0, core_id).start()
    init_copy(0).start()

    def fill_and_send(g, carry):
        fill(g)
        init_copy(g).start()
        return carry

    lax.fori_loop(1, GROUPS, fill_and_send, 0)
    loads[5].wait()
    loads[6].wait()

    def add_dir(d, acc):
        return acc + act_ref[pl.ds(pl.multiple_of(d * block, 8), block)]

    total = lax.fori_loop(0, dirs, add_dir, jnp.zeros((block, 128), jnp.float32), unroll=4)

    small_copy(0, core_id).wait_recv()
    other_c = small_recv[0]
    first = jnp.where(core1, other_c, mine_c)
    second = jnp.where(core1, mine_c, other_c)
    even = iota((block, 128), 0) % 2 == 0

    def rows_of(row):
        return jnp.where(
            even,
            jnp.broadcast_to(first[row : row + 1], (block, 128)),
            jnp.broadcast_to(second[row : row + 1], (block, 128)),
        )

    depth_w = rows_of(0)
    wet_w = rows_of(1)
    freq = (iota((block, 128), 0) // 2).astype(jnp.float32)
    shoal = jnp.tanh(depth_w * ((1.0 + 3.0 * freq / freqs) * 0.25))
    speed = 0.45 * shoal * wet_w
    fields[0] = speed
    fields[1] = 0.2 * (1.0 - shoal)

    def sum_rows(v):
        v8 = v[0:8]
        for i in range(1, block // 8):
            v8 = v8 + v[8 * i : 8 * i + 8]
        v8 = v8 + pltpu.roll(v8, 4, 0)
        return v8 + pltpu.roll(v8, 2, 0)

    scale = 1.0 / (dirs * freqs)
    orbital = wet_w[0:8] * (sum_rows(total * (1.0 - shoal * shoal)) * scale)
    flip = pltpu.roll(orbital, 1, 0)
    small_send[1] = jnp.where(core1, orbital, flip)
    small_copy(1, core_id).start()
    mine_o = jnp.where(core1, flip, orbital)

    my_rows = sub // 4 == jnp.full((8, 128), x, jnp.int32)

    def place_own(v):
        return jnp.where(core1, pltpu.roll(v, 4, 0), v)

    def unpack_pair(first, second, packed):
        turned = pltpu.roll(packed, 4, 0)
        return (
            jnp.where(my_rows, place_own(first), jnp.where(x1, packed, turned)),
            jnp.where(my_rows, place_own(second), jnp.where(x1, turned, packed)),
        )

    def send_edges(group, slot):
        rows = [conc[group, pl.ds(8 * u, 8)] for u in range(layers + 2)]
        row_send[slot, 0] = conc.at[group][pl.ds(7, 32, stride=8), :]
        row_send[slot, 1] = conc.at[group][pl.ds(0, 32, stride=8), :]
        right = jnp.zeros((8, 128), jnp.float32)
        left = jnp.zeros((8, 128), jnp.float32)
        for u, v in enumerate(rows):
            right = jnp.where(lane == u, roll(v, u + 1, 1), right)
            left = jnp.where(lane == u, roll(v, u, 1), left)
        col_send[slot, 0] = right
        col_send[slot, 1] = left
        for here, copy in edges:

            @pl.when(here)
            def _(copy=copy):
                copy(slot).start()

    def begin(group):
        init_copy(group).wait_recv()
        for k in range(classes):
            t0, t1 = unpack_pair(
                floc_ref[k, levels - 1 - 2 * group],
                floc_ref[k, levels - 2 - 2 * group],
                init_recv[group, pl.ds(8 * k, 8)],
            )
            conc[group, pl.ds(16 * k, 8)] = t0
            conc[group, pl.ds(16 * k + 8, 8)] = t1
        e, n = unpack_pair(east_tile, north_tile, init_recv[group, pl.ds(8 * classes, 8)])
        conc[group, pl.ds(8 * layers, 8)] = e
        conc[group, pl.ds(8 * layers + 8, 8)] = n
        s0, s1 = unpack_pair(
            shear_ref[levels - 1 - 2 * group],
            shear_ref[levels - 2 - 2 * group],
            init_recv[group, pl.ds(8 * classes + 8, 8)],
        )
        shear[group, 0] = 0.25 * s0
        shear[group, 1] = 0.25 * s1
        send_edges(group, group)

    begin(0)

    def flux(d, carry):
        start = pl.multiple_of(d * block, 8)
        flux_send[pl.ds(start, block)] = (trig_ref[0, d] * fields[0]) * act_ref[pl.ds(start, block)]
        return carry

    lax.fori_loop(0, dirs, flux, 0, unroll=4)

    for load in loads[7:]:
        load.wait()

    widen = jnp.where(iota((dirs, 128), 0) == iota((dirs, 128), 1), 1.0, 0.0)
    grow = jnp.dot(
        jnp.exp(wind_ref[...]),
        widen.astype(jnp.float32),
        precision=HIGHEST,
        preferred_element_type=jnp.float32,
    )
    pick = jnp.where(iota((block, freqs), 0) // 2 == iota((block, freqs), 1), 1.0, 0.0)
    grow = jnp.dot(
        pick.astype(jnp.float32), grow, precision=HIGHEST, preferred_element_type=jnp.float32
    )
    growth[...] = grow
    wave_sum[...] = jnp.zeros_like(wave_sum)


    small_copy(1, core_id).wait_recv()
    other_o = small_recv[1]
    coarse0 = jnp.where(core1, other_o, mine_o)[0:1]
    coarse1 = jnp.where(core1, mine_o, other_o)[0:1]
    tall = jnp.where(
        sub % 4 < 2, jnp.broadcast_to(coarse0, (8, 128)), jnp.broadcast_to(coarse1, (8, 128))
    )
    fine = jnp.where(
        low,
        jnp.dot(tall, spreadm[0], precision=HIGHEST, preferred_element_type=jnp.float32),
        jnp.dot(tall, spreadm[1], precision=HIGHEST, preferred_element_type=jnp.float32),
    )
    stress = 0.5 * (east_tile * east_tile + north_tile * north_tile) + fine
    excess_tile = wet * jnp.maximum(stress - threshold_stress, 0.0)
    small_send[2] = pack_pair(excess_tile, excess_tile, send_high)
    small_copy(2, pair_id).start()

    quarter = dirs // 4
    wide_lane = iota((block, 128), 1)

    def propagate(northward, q):
        def one(i, acc):
            d = q * quarter + i
            start = pl.multiple_of(d * block, 8)
            a = act_ref[pl.ds(start, block)]
            give = (trig_ref[1, d] * fields[0]) * a
            if northward:
                r = pltpu.roll(give, 1, 1)
                fix = jnp.where(even, 0.0, pltpu.roll(r, 1, 0))
                inflow = jnp.where(wide_lane == 0, fix, r)
            else:
                r = pltpu.roll(give, 127, 1)
                fix = jnp.where(even, pltpu.roll(r, block - 1, 0), 0.0)
                inflow = jnp.where(wide_lane == 127, fix, r)
            p = a - flux_send[pl.ds(start, block)] - give + flux_recv[pl.ds(start, block)] + inflow
            prop[pl.ds(start, block)] = p
            return acc + p

        wave_sum[...] = lax.fori_loop(0, quarter, one, wave_sum[...], unroll=3)

    def finish(q):
        turning = fields[1]

        def one(i, g):
            d = q * quarter + i
            before = jnp.where(d == 0, dirs - 1, d - 1)
            after = jnp.where(d == dirs - 1, 0, d + 1)
            p = prop[pl.ds(pl.multiple_of(d * block, 8), block)]
            pb = prop[pl.ds(pl.multiple_of(before * block, 8), block)]
            pa = prop[pl.ds(pl.multiple_of(after * block, 8), block)]
            spread = p + turning * (pb + pa - 2.0 * p)
            factor = jnp.broadcast_to(g[:, 0:1], (block, 128)) * decay_ref[...]
            act_out[pl.ds(pl.multiple_of(d * block, 8), block)] = spread * factor
            return pltpu.roll(g, 127, 1)

        growth[...] = lax.fori_loop(0, quarter, one, growth[...], unroll=3)

    def waves(t):
        @pl.when(t < CHUNKS)
        def _():
            for side in range(2):

                @pl.when(flux_goes[side])
                def _(side=side):
                    flux_copy(side, t).start()

        for part in range(4):

            @pl.when(t == CHUNKS + part)
            def _(part=part):
                @pl.when(flux_comes[part // 2])
                def _():
                    for i in range(CHUNKS // 2):
                        flux_copy(part // 2, part % 2 * (CHUNKS // 2) + i).wait_recv()

                propagate(part in (1, 2), part)

        @pl.when(t == CHUNKS + 4)
        def _():
            decay = jnp.exp(-0.5 * (sum_rows(wave_sum[...]) * scale))
            decay_ref[...] = jnp.concatenate([decay] * (block // 8), axis=0)

        @pl.when(t >= CHUNKS + 4)
        def _():
            finish(t - CHUNKS - 4)

    top = sub == 0
    bottom = sub == 7
    first_lane = lane == 0
    last_lane = lane == 127

    def step(t, carry):
        s = t // GROUPS
        g = t % GROUPS

        @pl.when(t < GROUPS - 1)
        def _():
            begin(g + 1)

        waves(t)

        for side, (here, (_, copy)) in enumerate(zip(arrives, edges)):

            @pl.when(here)
            def _(copy=copy):
                copy(t).wait_recv()

        from_low = row_recv.at[t, 0]
        from_high = row_recv.at[t, 1]
        from_left = col_recv[t, 0]
        from_right = col_recv[t, 1]

        def neighbours(u, v):
            west = jnp.where(top, from_low[pl.ds(u, 1)], pltpu.roll(v, 1, 0))
            east = jnp.where(bottom, from_high[pl.ds(u, 1)], pltpu.roll(v, 7, 0))
            south = jnp.where(first_lane, roll(from_left, 128 - u, 1), pltpu.roll(v, 1, 1))
            north = jnp.where(last_lane, roll(from_right, 127 - u, 1), pltpu.roll(v, 127, 1))
            return west, east, south, north

        @pl.when(t == 0)
        def _():
            e = conc[0, pl.ds(8 * layers, 8)]
            n = conc[0, pl.ds(8 * layers + 8, 8)]
            e_w, e_e, _, _ = neighbours(layers, e)
            _, _, n_s, n_n = neighbours(layers + 1, n)
            zero = jnp.zeros((8, 128), jnp.float32)

            def rate(v, edge, here):
                give = jnp.maximum(v, 0.0) + diffusion_rate
                return jnp.where(edge & same(here.astype(jnp.int32), 0), zero, give)

            coef[0] = 1.0 - (jnp.abs(e) + jnp.abs(n) + 4.0 * diffusion_rate)
            coef[1] = rate(e_w, top, has_low)
            coef[2] = rate(-e_e, bottom, has_high)
            coef[3] = rate(n_s, first_lane, has_down)
            coef[4] = rate(-n_n, last_lane, has_up)

        @pl.when(t == GROUPS - 1)
        def _():
            small_copy(2, pair_id).wait_recv()
            ex, _ = unpack_pair(excess_tile, excess_tile, small_recv[2])
            excess[...] = ex

        keep, c_w, c_e, c_s, c_n = [coef[i] for i in range(5)]
        for u in range(layers):
            v = conc[g, pl.ds(8 * u, 8)]
            west, east, south, north = neighbours(u, v)
            moved[pl.ds(8 * u, 8)] = (
                keep * v + (c_w * west + c_e * east) + (c_s * south + c_n * north)
            )
        sh = [shear[g, 0], shear[g, 1]]
        last_group = same(g, GROUPS - 1)
        ex = jnp.where(last_group, excess[...], 0.0)
        mv = [moved[pl.ds(8 * u, 8)] for u in range(layers)]
        for k in range(classes):
            mix = [None, None]
            brk = [None, None]
            for m in range(classes):
                a = agg_ref[k, m]
                b = brk_ref[k, m]
                for p in range(2):
                    v = mv[2 * m + p]
                    mix[p] = a * v if m == 0 else mix[p] + a * v
                    brk[p] = b * v if m == 0 else brk[p] + b * v
            r = [
                mv[2 * k + p] + sh[p] * mv[2 * k + p] * mix[p] + 0.25 * brk[p] for p in range(2)
            ]
            w = settling_ref[k]
            top_above = above[pl.ds(8 * k, 8)]
            conc[g, pl.ds(16 * k, 8)] = r[0] - w * r[0] + w * top_above
            conc[g, pl.ds(16 * k + 8, 8)] = r[1] - w * r[1] + w * r[0] + erosion_ref[k] * ex
            above[pl.ds(8 * k, 8)] = jnp.where(last_group, 0.0, r[1])

        @pl.when(s < SUBSTEPS - 1)
        def _():
            send_edges(g, t + GROUPS)

        @pl.when(s == SUBSTEPS - 1)
        def _():
            for k in range(classes):
                back_send[g, pl.ds(8 * k, 8)] = pack_pair(
                    conc[g, pl.ds(16 * k, 8)], conc[g, pl.ds(16 * k + 8, 8)], same(x, 0)
                )
            back_copy(g).start()

        return carry

    lax.fori_loop(0, SUBSTEPS * GROUPS, step, 0)

    own = sub // 4 == jnp.full((8, 128), own_half, jnp.int32)
    own1 = same(own_half, 1)

    def gather_back(g, carry):
        back_copy(g).wait_recv()
        for k in range(classes):
            packed = back_recv[g, pl.ds(8 * k, 8)]
            turned = pltpu.roll(packed, 4, 0)
            t0 = place_own(conc[g, pl.ds(16 * k, 8)])
            t1 = place_own(conc[g, pl.ds(16 * k + 8, 8)])
            floc_out[k, levels - 1 - 2 * g] = jnp.where(
                own, t0, jnp.where(own1, packed, turned)
            )
            floc_out[k, levels - 2 - 2 * g] = jnp.where(
                own, t1, jnp.where(own1, turned, packed)
            )
        return carry

    lax.fori_loop(0, GROUPS, gather_back, 0)

    small_copy(0, core_id).wait_send()
    small_copy(1, core_id).wait_send()
    small_copy(2, pair_id).wait_send()

    def drain_groups(g, carry):
        init_copy(g).wait_send()
        back_copy(g).wait_send()
        return carry

    lax.fori_loop(0, GROUPS, drain_groups, 0)

    def drain_edges(t, carry):
        for here, copy in edges:

            @pl.when(here)
            def _(copy=copy):
                copy(t).wait_send()

        return carry

    lax.fori_loop(0, SUBSTEPS * GROUPS, drain_edges, 0)

    for side in range(2):

        @pl.when(flux_goes[side])
        def _(side=side):
            lax.fori_loop(
                0, CHUNKS, lambda i, c: (flux_copy(side, i).wait_send(), c)[1], 0
            )


def halves(tile):
    rows = tile.shape[-2]
    split = tile.reshape(tile.shape[:-1] + (2, 128))
    return jnp.swapaxes(split, -3, -2).reshape(tile.shape[:-2] + (2 * rows, 128))


def unhalves(tile):
    rows = tile.shape[-2] // 2
    split = tile.reshape(tile.shape[:-2] + (2, rows, 128))
    return jnp.swapaxes(split, -3, -2).reshape(tile.shape[:-2] + (rows, 256))


def body(
    pairs,
    floc_conc,
    currents,
    water_depth,
    wet_mask,
    shear_rate,
    aggregation,
    breakup,
    settling,
    erosion,
    action_density,
    wind_growth,
):
    classes, levels = floc_conc.shape[:2]
    dirs, freqs = wind_growth.shape
    rows = dirs * freqs * 2
    angles = (np.arange(dirs) + 0.5) * (2.0 * math.pi / dirs) - 0.5 * math.pi
    trig = jnp.asarray(np.abs(np.stack([np.cos(angles), np.sin(angles)])).astype(np.float32))
    vmem = pl.BlockSpec(memory_space=pltpu.VMEM)
    hbm = pl.BlockSpec(memory_space=pltpu.HBM)
    S = pltpu.SMEM
    slots = SUBSTEPS * GROUPS
    f32 = jnp.float32
    V = pltpu.VMEM
    out_floc, out_act = pl.pallas_call(
        functools.partial(kernel, classes, levels, dirs, freqs, pairs),
        out_shape=(
            jax.ShapeDtypeStruct((classes, levels, 8, 128), f32),
            jax.ShapeDtypeStruct((rows, 128), f32),
        ),
        in_specs=[hbm] * 12,
        out_specs=(vmem, vmem),
        scratch_shapes=[
            V((GROUPS, 32 * 8, 128), f32),
            V((GROUPS, 2, 8, 128), f32),
            V((5, 8, 128), f32),
            V((8, 128), f32),
            V((classes * 8, 128), f32),
            V((classes * 16, 128), f32),
            V((GROUPS, classes * 8 + 16, 128), f32),
            V((GROUPS, classes * 8 + 16, 128), f32),
            V((slots, 2, 32, 128), f32),
            V((slots, 2, 32, 128), f32),
            V((slots, 2, 8, 128), f32),
            V((slots, 2, 8, 128), f32),
            V((GROUPS, classes * 8, 128), f32),
            V((GROUPS, classes * 8, 128), f32),
            V((3, 8, 128), f32),
            V((3, 8, 128), f32),
            V((rows, 128), f32),
            V((rows, 128), f32),
            V((rows, 128), f32),
            V((2, 2 * freqs, 128), f32),
            V((2 * freqs, 128), f32),
            V((2 * freqs, 128), f32),
            V((2 * freqs, 128), f32),
            V((classes, levels, 8, 128), f32),
            V((2, 8, 128), f32),
            V((8, 128), f32),
            V((8, 128), jnp.int32),
            V((levels, 8, 128), f32),
            S((classes, classes), f32),
            S((classes, classes), f32),
            S((classes,), f32),
            S((classes,), f32),
            V((rows, 128), f32),
            V((freqs, dirs), f32),
            S((2, dirs), f32),
            pltpu.SemaphoreType.DMA((12,)),
            pltpu.SemaphoreType.DMA((2, GROUPS)),
            pltpu.SemaphoreType.DMA((2, slots, 4)),
            pltpu.SemaphoreType.DMA((2, GROUPS)),
            pltpu.SemaphoreType.DMA((2, 3)),
            pltpu.SemaphoreType.DMA((2, 2, CHUNKS)),
        ],
        compiler_params=pltpu.CompilerParams(
            collective_id=0, has_side_effects=True, vmem_limit_bytes=60 * 1024 * 1024
        ),
    )(
        halves(floc_conc),
        halves(currents),
        halves(water_depth),
        halves(wet_mask),
        halves(shear_rate),
        aggregation,
        breakup,
        settling,
        erosion,
        action_density.reshape(rows, 128),
        wind_growth.T,
        trig,
    )
    return unhalves(out_floc), out_act.reshape(action_density.shape)


def solution(mesh):
    placed = (
        P(None, None, ("group", "along"), "cross"),
        P(None, ("group", "along"), "cross"),
        P(("group", "along"), "cross"),
        P(("group", "along"), "cross"),
        P(None, ("group", "along"), "cross"),
        P(),
        P(),
        P(),
        P(),
        P(None, None, ("group", "along", "cross"), None),
        P(),
    )
    return jax.shard_map(
        functools.partial(body, mesh.shape["along"] // 2),
        mesh=mesh,
        in_specs=placed,
        out_specs=(
            P(None, None, ("group", "along"), "cross"),
            P(None, None, ("group", "along", "cross"), None),
        ),
        check_vma=False,
    )
```

```python
import functools
import math

import jax
import jax.numpy as jnp
import numpy as np
from jax import lax
from jax.experimental import pallas as pl
from jax.experimental.pallas import tpu as pltpu
from jax.sharding import PartitionSpec as P

SUBSTEPS = 4
GROUPS = 4
CHUNKS = 8
diffusion_rate = 0.05
threshold_stress = 0.25
MESH = pl.DeviceIdType.MESH
HIGHEST = lax.Precision.HIGHEST


def roll(x, shift, axis):
    shift = shift % x.shape[axis]
    return x if shift == 0 else pltpu.roll(x, shift, axis)


def iota(shape, dim):
    return lax.broadcasted_iota(jnp.int32, shape, dim)


def kernel(
    classes,
    levels,
    dirs,
    freqs,
    pairs,
    floc_hbm,
    cur_hbm,
    depth_hbm,
    wet_hbm,
    shear_hbm,
    agg_hbm,
    brk_hbm,
    settling_hbm,
    erosion_hbm,
    act_hbm,
    wind_hbm,
    trig_hbm,
    floc_out,
    act_out,
    conc,
    shear,
    coef,
    excess,
    above,
    moved,
    init_send,
    init_recv,
    row_send,
    row_recv,
    col_send,
    col_recv,
    back_send,
    back_recv,
    small_send,
    small_recv,
    flux_send,
    flux_recv,
    prop,
    fields,
    growth,
    wave_sum,
    decay_ref,
    floc_ref,
    cur_ref,
    depth_ref,
    wet_ref,
    shear_ref,
    agg_ref,
    brk_ref,
    settling_ref,
    erosion_ref,
    act_ref,
    wind_ref,
    trig_ref,
    load_sems,
    init_sems,
    edge_sems,
    back_sems,
    small_sems,
    flux_sems,
):
    along = lax.axis_index("along")
    core = lax.axis_index("cross")
    x = along % 2
    z = along // 2
    own_half = (x + core) % 2
    per = levels // GROUPS
    layers = classes * per
    sub = iota((8, 128), 0)
    lane = iota((8, 128), 1)
    low = sub < 4

    def same(scalar, value):
        return jnp.full((8, 128), scalar, jnp.int32) == value

    core1 = same(core, 1)
    x1 = same(x, 1)
    pair_id = {"along": along + 1 - 2 * x}
    core_id = {"cross": 1 - core}
    place = x + core * (3 - 2 * x)
    outer_wave = jnp.where(core == 1, along + 1, along - 1)
    has_outer = (outer_wave >= 0) & (outer_wave < 2 * pairs)
    outer_id = {"along": outer_wave, "cross": 1 - core}
    has_low = z > 0
    has_high = z < pairs - 1
    low_id = {"along": along - 2}
    high_id = {"along": along + 2}

    loads = [
        pltpu.make_async_copy(src, dst, load_sems.at[i])
        for i, (src, dst) in enumerate(
            (
                (wet_hbm, wet_ref),
                (cur_hbm, cur_ref),
                (depth_hbm, depth_ref),
                (shear_hbm, shear_ref),
                (floc_hbm, floc_ref),
                (act_hbm, act_ref),
                (trig_hbm, trig_ref),
                (agg_hbm, agg_ref),
                (brk_hbm, brk_ref),
                (settling_hbm, settling_ref),
                (erosion_hbm, erosion_ref),
                (wind_hbm, wind_ref),
            )
        )
    ]
    barrier = pltpu.get_barrier_semaphore()
    pl.semaphore_signal(barrier, inc=1, device_id=pair_id, device_id_type=MESH)
    pl.semaphore_signal(barrier, inc=1, device_id=core_id, device_id_type=MESH)

    @pl.when(has_low)
    def _():
        pl.semaphore_signal(barrier, inc=1, device_id=low_id, device_id_type=MESH)

    @pl.when(has_high)
    def _():
        pl.semaphore_signal(barrier, inc=1, device_id=high_id, device_id_type=MESH)

    @pl.when(has_outer)
    def _():
        pl.semaphore_signal(barrier, inc=1, device_id=outer_id, device_id_type=MESH)

    for load in loads:
        load.start()
    for load in loads[:4]:
        load.wait()

    wet = wet_ref[...].astype(jnp.float32)
    east_tile = cur_ref[0] * wet
    north_tile = cur_ref[1] * wet
    depth = depth_ref[...]

    def pack_pair(first, second, take_high):
        return jnp.where(
            take_high,
            jnp.where(low, pltpu.roll(first, 4, 0), second),
            jnp.where(low, first, pltpu.roll(second, 4, 0)),
        )

    send_high = same(own_half, 0)

    def fill(group):
        for k in range(classes):
            init_send[group, pl.ds(8 * k, 8)] = pack_pair(
                floc_ref[k, levels - 1 - 2 * group], floc_ref[k, levels - 2 - 2 * group], send_high
            )
        init_send[group, pl.ds(8 * classes, 8)] = pack_pair(east_tile, north_tile, send_high)
        init_send[group, pl.ds(8 * classes + 8, 8)] = pack_pair(
            shear_ref[levels - 1 - 2 * group], shear_ref[levels - 2 - 2 * group], send_high
        )

    def init_copy(group):
        return pltpu.make_async_remote_copy(
            src_ref=init_send.at[group],
            dst_ref=init_recv.at[group],
            send_sem=init_sems.at[0, group],
            recv_sem=init_sems.at[1, group],
            device_id=pair_id,
            device_id_type=MESH,
        )

    def back_copy(group):
        return pltpu.make_async_remote_copy(
            src_ref=back_send.at[group],
            dst_ref=back_recv.at[group],
            send_sem=back_sems.at[0, group],
            recv_sem=back_sems.at[1, group],
            device_id=pair_id,
            device_id_type=MESH,
        )

    def small_copy(slot, target):
        return pltpu.make_async_remote_copy(
            src_ref=small_send.at[slot],
            dst_ref=small_recv.at[slot],
            send_sem=small_sems.at[0, slot],
            recv_sem=small_sems.at[1, slot],
            device_id=target,
            device_id_type=MESH,
        )

    def row_copy(slot, side, target):
        return pltpu.make_async_remote_copy(
            src_ref=row_send.at[slot, side],
            dst_ref=row_recv.at[slot, side],
            send_sem=edge_sems.at[0, slot, side],
            recv_sem=edge_sems.at[1, slot, side],
            device_id=target,
            device_id_type=MESH,
        )

    def col_copy(slot, side, target):
        return pltpu.make_async_remote_copy(
            src_ref=col_send.at[slot, side],
            dst_ref=col_recv.at[slot, side],
            send_sem=edge_sems.at[0, slot, 2 + side],
            recv_sem=edge_sems.at[1, slot, 2 + side],
            device_id=target,
            device_id_type=MESH,
        )

    up_is_pair = (place == 0) | (place == 2)
    down_is_pair = (place == 1) | (place == 3)
    pair_along = along + 1 - 2 * x
    up_id = {
        "along": jnp.where(up_is_pair, pair_along, along),
        "cross": jnp.where(up_is_pair, core, 1 - core),
    }
    down_id = {
        "along": jnp.where(down_is_pair, pair_along, along),
        "cross": jnp.where(down_is_pair, core, 1 - core),
    }
    has_up = place < 3
    has_down = place > 0

    edges = (
        (has_high, functools.partial(row_copy, side=0, target=high_id)),
        (has_low, functools.partial(row_copy, side=1, target=low_id)),
        (has_up, functools.partial(col_copy, side=0, target=up_id)),
        (has_down, functools.partial(col_copy, side=1, target=down_id)),
    )
    arrives = (has_low, has_high, has_down, has_up)

    a_in = iota((128, 128), 0)
    b_in = iota((128, 128), 1)
    gather = [jnp.where(a_in // 2 + 64 * j == b_in, 0.25, 0.0).astype(jnp.float32) for j in range(2)]
    spreadm = [jnp.where(a_in == 64 * j + b_in // 2, 1.0, 0.0).astype(jnp.float32) for j in range(2)]

    def coarse(v):
        v = v + pltpu.roll(v, 7, 0)
        c0 = jnp.dot(v, gather[0], precision=HIGHEST, preferred_element_type=jnp.float32)
        c1 = jnp.dot(v, gather[1], precision=HIGHEST, preferred_element_type=jnp.float32)
        return c0 + pltpu.roll(c1, 4, 0)

    depth_c = coarse(depth)
    wet_c = coarse(wet)
    both = jnp.where(sub % 2 == 0, depth_c, pltpu.roll(wet_c, 1, 0))
    mine_c = jnp.where(core1, pltpu.roll(both, 6, 0), both)
    small_send[0] = jnp.where(core1, both, pltpu.roll(both, 6, 0))

    for side, here in enumerate(arrives):

        @pl.when(jnp.logical_not(here))
        def _(side=side):
            def clear(slot, carry):
                if side < 2:
                    row_recv[slot, side] = jnp.zeros((32, 128), jnp.float32)
                else:
                    col_recv[slot, side - 2] = jnp.zeros((8, 128), jnp.float32)
                return carry

            lax.fori_loop(0, SUBSTEPS * GROUPS, clear, 0)

    half_rows = flux_recv.shape[0] // 2
    block = 2 * freqs
    chunk_rows = half_rows // CHUNKS
    flux_goes = ((core == 0) | has_outer, (core == 1) | has_outer)
    flux_comes = ((core == 1) | has_outer, (core == 0) | has_outer)
    flux_along = (
        jnp.where(core == 0, along, along + 1),
        jnp.where(core == 1, along, along - 1),
    )

    def flux_copy(side, chunk):
        start = side * half_rows + chunk * chunk_rows
        part = pl.ds(pl.multiple_of(start, 8), chunk_rows)
        return pltpu.make_async_remote_copy(
            src_ref=flux_send.at[part],
            dst_ref=flux_recv.at[part],
            send_sem=flux_sems.at[0, side, chunk],
            recv_sem=flux_sems.at[1, side, chunk],
            device_id={"along": flux_along[side], "cross": 1 - core},
            device_id_type=MESH,
        )


    @pl.when(jnp.logical_not(has_outer))
    def _():
        def clear(d, carry):
            start = pl.multiple_of(core * half_rows + d * block, 8)
            flux_recv[pl.ds(start, block)] = jnp.zeros((block, 128), jnp.float32)
            return carry

        lax.fori_loop(0, dirs // 2, clear, 0)

    above[...] = jnp.zeros_like(above)
    excess[...] = jnp.zeros_like(excess)

    loads[4].wait()
    fill(0)
    waits = 2 + has_low.astype(jnp.int32) + has_high.astype(jnp.int32) + has_outer.astype(jnp.int32)
    pl.semaphore_wait(barrier, waits)
    small_copy(0, core_id).start()
    init_copy(0).start()

    def fill_and_send(g, carry):
        fill(g)
        init_copy(g).start()
        return carry

    lax.fori_loop(1, GROUPS, fill_and_send, 0)
    loads[5].wait()
    loads[6].wait()

    def add_dir(d, acc):
        return acc + act_ref[pl.ds(pl.multiple_of(d * block, 8), block)]

    total = lax.fori_loop(0, dirs, add_dir, jnp.zeros((block, 128), jnp.float32), unroll=4)

    small_copy(0, core_id).wait_recv()
    other_c = small_recv[0]
    first = jnp.where(core1, other_c, mine_c)
    second = jnp.where(core1, mine_c, other_c)
    even = iota((block, 128), 0) % 2 == 0

    def rows_of(row):
        return jnp.where(
            even,
            jnp.broadcast_to(first[row : row + 1], (block, 128)),
            jnp.broadcast_to(second[row : row + 1], (block, 128)),
        )

    depth_w = rows_of(0)
    wet_w = rows_of(1)
    freq = (iota((block, 128), 0) // 2).astype(jnp.float32)
    shoal = jnp.tanh(depth_w * ((1.0 + 3.0 * freq / freqs) * 0.25))
    speed = 0.45 * shoal * wet_w
    fields[0] = speed
    fields[1] = 0.2 * (1.0 - shoal)

    def sum_rows(v):
        v8 = v[0:8]
        for i in range(1, block // 8):
            v8 = v8 + v[8 * i : 8 * i + 8]
        v8 = v8 + pltpu.roll(v8, 4, 0)
        return v8 + pltpu.roll(v8, 2, 0)

    scale = 1.0 / (dirs * freqs)
    orbital = wet_w[0:8] * (sum_rows(total * (1.0 - shoal * shoal)) * scale)
    flip = pltpu.roll(orbital, 1, 0)
    small_send[1] = jnp.where(core1, orbital, flip)
    small_copy(1, core_id).start()
    mine_o = jnp.where(core1, flip, orbital)

    my_rows = sub // 4 == jnp.full((8, 128), x, jnp.int32)

    def place_own(v):
        return jnp.where(core1, pltpu.roll(v, 4, 0), v)

    def unpack_pair(first, second, packed):
        turned = pltpu.roll(packed, 4, 0)
        return (
            jnp.where(my_rows, place_own(first), jnp.where(x1, packed, turned)),
            jnp.where(my_rows, place_own(second), jnp.where(x1, turned, packed)),
        )

    def send_edges(group, slot):
        rows = [conc[group, pl.ds(8 * u, 8)] for u in range(layers + 2)]
        row_send[slot, 0] = conc.at[group][pl.ds(7, 32, stride=8), :]
        row_send[slot, 1] = conc.at[group][pl.ds(0, 32, stride=8), :]
        for here, copy in edges[:2]:

            @pl.when(here)
            def _(copy=copy):
                copy(slot).start()

        right = jnp.zeros((8, 128), jnp.float32)
        left = jnp.zeros((8, 128), jnp.float32)
        for u, v in enumerate(rows):
            right = jnp.where(lane == u, roll(v, u + 1, 1), right)
            left = jnp.where(lane == u, roll(v, u, 1), left)
        col_send[slot, 0] = right
        col_send[slot, 1] = left
        for here, copy in edges[2:]:

            @pl.when(here)
            def _(copy=copy):
                copy(slot).start()

    def begin(group):
        init_copy(group).wait()
        for k in range(classes):
            t0, t1 = unpack_pair(
                floc_ref[k, levels - 1 - 2 * group],
                floc_ref[k, levels - 2 - 2 * group],
                init_recv[group, pl.ds(8 * k, 8)],
            )
            conc[group, pl.ds(16 * k, 8)] = t0
            conc[group, pl.ds(16 * k + 8, 8)] = t1
        e, n = unpack_pair(east_tile, north_tile, init_recv[group, pl.ds(8 * classes, 8)])
        conc[group, pl.ds(8 * layers, 8)] = e
        conc[group, pl.ds(8 * layers + 8, 8)] = n
        s0, s1 = unpack_pair(
            shear_ref[levels - 1 - 2 * group],
            shear_ref[levels - 2 - 2 * group],
            init_recv[group, pl.ds(8 * classes + 8, 8)],
        )
        shear[group, 0] = 0.25 * s0
        shear[group, 1] = 0.25 * s1
        send_edges(group, group)

    begin(0)

    def flux(d, carry):
        start = pl.multiple_of(d * block, 8)
        flux_send[pl.ds(start, block)] = (trig_ref[0, d] * fields[0]) * act_ref[pl.ds(start, block)]
        return carry

    lax.fori_loop(0, dirs, flux, 0, unroll=4)

    for load in loads[7:]:
        load.wait()

    widen = jnp.where(iota((dirs, 128), 0) == iota((dirs, 128), 1), 1.0, 0.0)
    grow = jnp.dot(
        jnp.exp(wind_ref[...]),
        widen.astype(jnp.float32),
        precision=HIGHEST,
        preferred_element_type=jnp.float32,
    )
    pick = jnp.where(iota((block, freqs), 0) // 2 == iota((block, freqs), 1), 1.0, 0.0)
    grow = jnp.dot(
        pick.astype(jnp.float32), grow, precision=HIGHEST, preferred_element_type=jnp.float32
    )
    growth[...] = grow
    wave_sum[...] = jnp.zeros_like(wave_sum)


    small_copy(1, core_id).wait_recv()
    other_o = small_recv[1]
    coarse0 = jnp.where(core1, other_o, mine_o)[0:1]
    coarse1 = jnp.where(core1, mine_o, other_o)[0:1]
    tall = jnp.where(
        sub % 4 < 2, jnp.broadcast_to(coarse0, (8, 128)), jnp.broadcast_to(coarse1, (8, 128))
    )
    fine = jnp.where(
        low,
        jnp.dot(tall, spreadm[0], precision=HIGHEST, preferred_element_type=jnp.float32),
        jnp.dot(tall, spreadm[1], precision=HIGHEST, preferred_element_type=jnp.float32),
    )
    stress = 0.5 * (east_tile * east_tile + north_tile * north_tile) + fine
    excess_tile = wet * jnp.maximum(stress - threshold_stress, 0.0)
    small_send[2] = pack_pair(excess_tile, excess_tile, send_high)
    small_copy(2, pair_id).start()

    quarter = dirs // 4
    wide_lane = iota((block, 128), 1)

    def propagate(northward, q):
        def one(i, acc):
            d = q * quarter + i
            start = pl.multiple_of(d * block, 8)
            a = act_ref[pl.ds(start, block)]
            give = (trig_ref[1, d] * fields[0]) * a
            if northward:
                r = pltpu.roll(give, 1, 1)
                fix = jnp.where(even, 0.0, pltpu.roll(r, 1, 0))
                inflow = jnp.where(wide_lane == 0, fix, r)
            else:
                r = pltpu.roll(give, 127, 1)
                fix = jnp.where(even, pltpu.roll(r, block - 1, 0), 0.0)
                inflow = jnp.where(wide_lane == 127, fix, r)
            p = a - flux_send[pl.ds(start, block)] - give + flux_recv[pl.ds(start, block)] + inflow
            prop[pl.ds(start, block)] = p
            return acc + p

        wave_sum[...] = lax.fori_loop(0, quarter, one, wave_sum[...], unroll=3)

    def finish(q):
        turning = fields[1]

        def one(i, g):
            d = q * quarter + i
            before = jnp.where(d == 0, dirs - 1, d - 1)
            after = jnp.where(d == dirs - 1, 0, d + 1)
            p = prop[pl.ds(pl.multiple_of(d * block, 8), block)]
            pb = prop[pl.ds(pl.multiple_of(before * block, 8), block)]
            pa = prop[pl.ds(pl.multiple_of(after * block, 8), block)]
            spread = p + turning * (pb + pa - 2.0 * p)
            factor = jnp.broadcast_to(g[:, 0:1], (block, 128)) * decay_ref[...]
            act_out[pl.ds(pl.multiple_of(d * block, 8), block)] = spread * factor
            return pltpu.roll(g, 127, 1)

        growth[...] = lax.fori_loop(0, quarter, one, growth[...], unroll=3)

    def waves(t):
        @pl.when(t < CHUNKS)
        def _():
            for side in range(2):

                @pl.when(flux_goes[side])
                def _(side=side):
                    flux_copy(side, t).start()

        for part in range(4):

            @pl.when(t == CHUNKS + part)
            def _(part=part):
                @pl.when(flux_comes[part // 2])
                def _():
                    for i in range(CHUNKS // 2):
                        flux_copy(part // 2, part % 2 * (CHUNKS // 2) + i).wait_recv()

                propagate(part in (1, 2), part)

        @pl.when(t >= CHUNKS)
        def _():
            for side in range(2):

                @pl.when(flux_goes[side])
                def _(side=side):
                    flux_copy(side, t - CHUNKS).wait_send()

        @pl.when(t == CHUNKS + 4)
        def _():
            decay = jnp.exp(-0.5 * (sum_rows(wave_sum[...]) * scale))
            decay_ref[...] = jnp.concatenate([decay] * (block // 8), axis=0)

        @pl.when(t >= CHUNKS + 4)
        def _():
            finish(t - CHUNKS - 4)

    top = sub == 0
    bottom = sub == 7
    first_lane = lane == 0
    last_lane = lane == 127

    def step(t, carry):
        s = t // GROUPS
        g = t % GROUPS

        @pl.when(t < GROUPS - 1)
        def _():
            begin(g + 1)

        waves(t)

        for side, (here, (_, copy)) in enumerate(zip(arrives, edges)):

            @pl.when(here)
            def _(copy=copy):
                copy(t).wait_recv()

            @pl.when(edges[side][0])
            def _(copy=copy):
                copy(t).wait_send()

        from_low = row_recv.at[t, 0]
        from_high = row_recv.at[t, 1]
        from_left = col_recv[t, 0]
        from_right = col_recv[t, 1]

        def neighbours(u, v):
            west = jnp.where(top, from_low[pl.ds(u, 1)], pltpu.roll(v, 1, 0))
            east = jnp.where(bottom, from_high[pl.ds(u, 1)], pltpu.roll(v, 7, 0))
            south = jnp.where(first_lane, roll(from_left, 128 - u, 1), pltpu.roll(v, 1, 1))
            north = jnp.where(last_lane, roll(from_right, 127 - u, 1), pltpu.roll(v, 127, 1))
            return west, east, south, north

        @pl.when(t == 0)
        def _():
            e = conc[0, pl.ds(8 * layers, 8)]
            n = conc[0, pl.ds(8 * layers + 8, 8)]
            e_w, e_e, _, _ = neighbours(layers, e)
            _, _, n_s, n_n = neighbours(layers + 1, n)
            zero = jnp.zeros((8, 128), jnp.float32)

            def rate(v, edge, here):
                give = jnp.maximum(v, 0.0) + diffusion_rate
                return jnp.where(edge & same(here.astype(jnp.int32), 0), zero, give)

            coef[0] = 1.0 - (jnp.abs(e) + jnp.abs(n) + 4.0 * diffusion_rate)
            coef[1] = rate(e_w, top, has_low)
            coef[2] = rate(-e_e, bottom, has_high)
            coef[3] = rate(n_s, first_lane, has_down)
            coef[4] = rate(-n_n, last_lane, has_up)

        @pl.when(t == GROUPS - 1)
        def _():
            small_copy(2, pair_id).wait_recv()
            ex, _ = unpack_pair(excess_tile, excess_tile, small_recv[2])
            excess[...] = ex

        keep, c_w, c_e, c_s, c_n = [coef[i] for i in range(5)]
        for u in range(layers):
            v = conc[g, pl.ds(8 * u, 8)]
            west, east, south, north = neighbours(u, v)
            moved[pl.ds(8 * u, 8)] = (
                keep * v + (c_w * west + c_e * east) + (c_s * south + c_n * north)
            )
        sh = [shear[g, 0], shear[g, 1]]
        last_group = same(g, GROUPS - 1)
        ex = jnp.where(last_group, excess[...], 0.0)
        mv = [moved[pl.ds(8 * u, 8)] for u in range(layers)]
        for k in range(classes):
            mix = [None, None]
            brk = [None, None]
            for m in range(classes):
                a = agg_ref[k, m]
                b = brk_ref[k, m]
                for p in range(2):
                    v = mv[2 * m + p]
                    mix[p] = a * v if m == 0 else mix[p] + a * v
                    brk[p] = b * v if m == 0 else brk[p] + b * v
            r = [
                mv[2 * k + p] + sh[p] * mv[2 * k + p] * mix[p] + 0.25 * brk[p] for p in range(2)
            ]
            w = settling_ref[k]
            top_above = above[pl.ds(8 * k, 8)]
            conc[g, pl.ds(16 * k, 8)] = r[0] - w * r[0] + w * top_above
            conc[g, pl.ds(16 * k + 8, 8)] = r[1] - w * r[1] + w * r[0] + erosion_ref[k] * ex
            above[pl.ds(8 * k, 8)] = jnp.where(last_group, 0.0, r[1])

        @pl.when(s < SUBSTEPS - 1)
        def _():
            send_edges(g, t + GROUPS)

        @pl.when(s == SUBSTEPS - 1)
        def _():
            for k in range(classes):
                back_send[g, pl.ds(8 * k, 8)] = pack_pair(
                    conc[g, pl.ds(16 * k, 8)], conc[g, pl.ds(16 * k + 8, 8)], same(x, 0)
                )
            back_copy(g).start()

        return carry

    lax.fori_loop(0, SUBSTEPS * GROUPS, step, 0)

    own = sub // 4 == jnp.full((8, 128), own_half, jnp.int32)
    own1 = same(own_half, 1)

    def gather_back(g, carry):
        back_copy(g).wait_recv()
        for k in range(classes):
            packed = back_recv[g, pl.ds(8 * k, 8)]
            turned = pltpu.roll(packed, 4, 0)
            t0 = place_own(conc[g, pl.ds(16 * k, 8)])
            t1 = place_own(conc[g, pl.ds(16 * k + 8, 8)])
            floc_out[k, levels - 1 - 2 * g] = jnp.where(
                own, t0, jnp.where(own1, packed, turned)
            )
            floc_out[k, levels - 2 - 2 * g] = jnp.where(
                own, t1, jnp.where(own1, turned, packed)
            )
        return carry

    lax.fori_loop(0, GROUPS, gather_back, 0)

    small_copy(0, core_id).wait_send()
    small_copy(1, core_id).wait_send()
    small_copy(2, pair_id).wait_send()

    def drain_groups(g, carry):
        back_copy(g).wait_send()
        return carry

    lax.fori_loop(0, GROUPS, drain_groups, 0)


def halves(tile):
    rows = tile.shape[-2]
    split = tile.reshape(tile.shape[:-1] + (2, 128))
    return jnp.swapaxes(split, -3, -2).reshape(tile.shape[:-2] + (2 * rows, 128))


def unhalves(tile):
    rows = tile.shape[-2] // 2
    split = tile.reshape(tile.shape[:-2] + (2, rows, 128))
    return jnp.swapaxes(split, -3, -2).reshape(tile.shape[:-2] + (rows, 256))


def body(
    pairs,
    floc_conc,
    currents,
    water_depth,
    wet_mask,
    shear_rate,
    aggregation,
    breakup,
    settling,
    erosion,
    action_density,
    wind_growth,
):
    classes, levels = floc_conc.shape[:2]
    dirs, freqs = wind_growth.shape
    rows = dirs * freqs * 2
    angles = (np.arange(dirs) + 0.5) * (2.0 * math.pi / dirs) - 0.5 * math.pi
    trig = jnp.asarray(np.abs(np.stack([np.cos(angles), np.sin(angles)])).astype(np.float32))
    vmem = pl.BlockSpec(memory_space=pltpu.VMEM)
    hbm = pl.BlockSpec(memory_space=pltpu.HBM)
    S = pltpu.SMEM
    slots = SUBSTEPS * GROUPS
    f32 = jnp.float32
    V = pltpu.VMEM
    out_floc, out_act = pl.pallas_call(
        functools.partial(kernel, classes, levels, dirs, freqs, pairs),
        out_shape=(
            jax.ShapeDtypeStruct((classes, levels, 8, 128), f32),
            jax.ShapeDtypeStruct((rows, 128), f32),
        ),
        in_specs=[hbm] * 12,
        out_specs=(vmem, vmem),
        scratch_shapes=[
            V((GROUPS, 33 * 8, 128), f32),
            V((GROUPS, 2, 8, 128), f32),
            V((5, 8, 128), f32),
            V((8, 128), f32),
            V((classes * 8, 128), f32),
            V((classes * 16, 128), f32),
            V((GROUPS, classes * 8 + 16, 128), f32),
            V((GROUPS, classes * 8 + 16, 128), f32),
            V((slots, 2, 32, 128), f32),
            V((slots, 2, 32, 128), f32),
            V((slots, 2, 8, 128), f32),
            V((slots, 2, 8, 128), f32),
            V((GROUPS, classes * 8, 128), f32),
            V((GROUPS, classes * 8, 128), f32),
            V((3, 8, 128), f32),
            V((3, 8, 128), f32),
            V((rows, 128), f32),
            V((rows, 128), f32),
            V((rows, 128), f32),
            V((2, 2 * freqs, 128), f32),
            V((2 * freqs, 128), f32),
            V((2 * freqs, 128), f32),
            V((2 * freqs, 128), f32),
            V((classes, levels, 8, 128), f32),
            V((2, 8, 128), f32),
            V((8, 128), f32),
            V((8, 128), jnp.int32),
            V((levels, 8, 128), f32),
            S((classes, classes), f32),
            S((classes, classes), f32),
            S((classes,), f32),
            S((classes,), f32),
            V((rows, 128), f32),
            V((freqs, dirs), f32),
            S((2, dirs), f32),
            pltpu.SemaphoreType.DMA((12,)),
            pltpu.SemaphoreType.DMA((2, GROUPS)),
            pltpu.SemaphoreType.DMA((2, slots, 4)),
            pltpu.SemaphoreType.DMA((2, GROUPS)),
            pltpu.SemaphoreType.DMA((2, 3)),
            pltpu.SemaphoreType.DMA((2, 2, CHUNKS)),
        ],
        compiler_params=pltpu.CompilerParams(
            collective_id=0, has_side_effects=True, vmem_limit_bytes=60 * 1024 * 1024
        ),
    )(
        halves(floc_conc),
        halves(currents),
        halves(water_depth),
        halves(wet_mask),
        halves(shear_rate),
        aggregation,
        breakup,
        settling,
        erosion,
        action_density.reshape(rows, 128),
        wind_growth.T,
        trig,
    )
    return unhalves(out_floc), out_act.reshape(action_density.shape)


def solution(mesh):
    placed = (
        P(None, None, ("group", "along"), "cross"),
        P(None, ("group", "along"), "cross"),
        P(("group", "along"), "cross"),
        P(("group", "along"), "cross"),
        P(None, ("group", "along"), "cross"),
        P(),
        P(),
        P(),
        P(),
        P(None, None, ("group", "along", "cross"), None),
        P(),
    )
    return jax.shard_map(
        functools.partial(body, mesh.shape["along"] // 2),
        mesh=mesh,
        in_specs=placed,
        out_specs=(
            P(None, None, ("group", "along"), "cross"),
            P(None, None, ("group", "along", "cross"), None),
        ),
        check_vma=False,
    )
```
